128 devices in a mesh: group: 8 (over z, core), tp: 16 (over x, y).
Axes of the slice: x: 4, y: 4, z: 4, core: 2. Of those that a mesh axis runs over, the one named last changes fastest.
Arguments:
- hidden_inputs: bfloat16 [3072, 2, 8192], P('group', None, 'tp'), may hold values from -6 to 6
- base_matrix: bfloat16 [8192, 8192], P(None, 'tp'), may hold values from -0.0625 to 0.0625
- adapter_down: bfloat16 [64, 64, 8192], P('group', None, 'tp'), may hold values from -0.0625 to 0.0625
- adapter_up: bfloat16 [64, 64, 8192], P('group', None, 'tp'), may hold values from -0.75 to 0.75
- adapter_ranks: int32 [64], replicated, may hold values from 16 to 64
- adapter_pages: int32 [64], replicated, may hold values from 0 to 63, as said below
- row_adapters: int32 [3072], P('group'), may hold values from 0 to 63, as said below
Outputs:
- adapted_rows: bfloat16 [3072, 2, 8192], P('group', None, 'tp')
The draws below stay inside these ranges and needn't reach their ends.
Inputs may be any that keep to these rules, and one draw needn't show every extreme that they name: `adapter_pages`: a permutation: every adapter has its own page slot; slot s lies with group s // 8. `row_adapters`: in each group's aligned block of 384 rows, at most 96 rows name adapters whose page slots lie with any one group, and exactly 96 rows do so for some group in every block.
All inputs are finite; a program needn't handle non-finite values.
Results may differ from the reference program's by a relative error of at most 0.0044.
Values may be sent and summed in bfloat16 or wider, within the bound.
No kernel may reach another device: no remote copies, remote signals or barrier semaphores. Data moves between devices by JAX's collectives and lax.ppermute only.
A program may use at most 128 MiB of HBM per device.

```python
import jax
import jax.numpy as jnp
from jax import lax

MODEL_WIDTH = 8192
MAXIMUM_RANK = 64
STEPS = 2
ROWS_DEV = 384
SLOTS = 8
ROWS = 3072
ADAPTER_TOTAL = 64


def shared_slots(key):
    return jax.random.permutation(key, ADAPTER_TOTAL).astype(jnp.int32)


def draw_adapter_pages(key, part):
    slot_of = shared_slots(key)
    return slot_of


def draw_row_adapters(key, part):
    slot_of = shared_slots(key)
    key = jax.random.fold_in(key, 7)
    holders = ADAPTER_TOTAL // SLOTS
    even_share = ROWS_DEV // holders
    adapter_at = jnp.argsort(slot_of, stable=True).astype(jnp.int32)

    def draw_block(block_key):
        key_giver, key_taker, key_order, key_slot = jax.random.split(block_key, 4)
        giver_group = jax.random.randint(key_giver, (), 0, holders)
        taker_group = (giver_group + jax.random.randint(key_taker, (), 1, holders)) % holders
        counts = jnp.full((holders,), even_share, jnp.int32)
        counts = counts.at[giver_group].add(-even_share).at[taker_group].add(even_share)
        destination = jnp.repeat(jnp.arange(holders, dtype=jnp.int32), counts, total_repeat_length=ROWS_DEV)
        destination = jax.random.permutation(key_order, destination)
        local_slot = jax.random.randint(key_slot, (ROWS_DEV,), 0, SLOTS)
        return adapter_at[destination * SLOTS + local_slot]
    block_keys = jax.random.split(key, holders)
    return jax.vmap(draw_block)(block_keys).reshape(-1).astype(jnp.int32)


def touch_ends(drawn, key, least, high):
    longest = drawn.shape.index(max(drawn.shape))
    spots = []
    for shift in (0, 1):
        where = [jax.random.randint(jax.random.fold_in(key, axis), (), 0, length) for axis, length in enumerate(drawn.shape)]
        where[longest] = (where[longest] + shift) % drawn.shape[longest]
        spots.append(tuple(where))
    return drawn.at[spots[0]].set(least).at[spots[1]].set(high)


def block_scale(own_key, shape, shards, smallest, high):
    def one(position, shards_of):
        heights = jax.random.uniform(jax.random.fold_in(jax.random.fold_in(own_key, 6), position), (shards_of,), jnp.float32, smallest / len(shards), high / len(shards))
        return jnp.repeat(jnp.exp(heights), shape[position] // shards_of).reshape((-1,) + (1,) * (len(shape) - position - 1))

    loudness = one(*shards[0])
    for cut in shards[1:]:
        loudness = loudness * one(*cut)
    return loudness


def centred(own_key, shape, width, reach, pieces=(), kind=jnp.bfloat16):
    gain = block_scale(own_key, shape, pieces, -0.22, 0.18) if pieces else 1.0
    values = jax.random.normal(own_key, shape, jnp.float32) * width * gain
    return jnp.minimum(jnp.maximum(values, -reach), reach).astype(kind)


def setup_inputs(seed: int = 0) -> dict:
    key_list = jax.random.split(jax.random.key(seed), 8)
    hidden_inputs = centred(key_list[0], (ROWS, STEPS, MODEL_WIDTH), 1.0, 6.0, ((0, 8), (2, 16)))
    base_matrix = centred(key_list[1], (MODEL_WIDTH, MODEL_WIDTH), MODEL_WIDTH ** -0.5, 0.0625, ((1, 16),))
    adapter_down = centred(key_list[2], (ADAPTER_TOTAL, MAXIMUM_RANK, MODEL_WIDTH), MODEL_WIDTH ** -0.5, 0.0625, ((0, 8), (2, 16)))
    adapter_up = centred(key_list[3], (ADAPTER_TOTAL, MAXIMUM_RANK, MODEL_WIDTH), MAXIMUM_RANK ** -0.5, 0.75, ((0, 8), (2, 16)))
    adapter_ranks = touch_ends(jax.random.randint(key_list[4], (ADAPTER_TOTAL,), MAXIMUM_RANK // 4, MAXIMUM_RANK + 1), jax.random.fold_in(key_list[4], 1), MAXIMUM_RANK // 4, MAXIMUM_RANK).astype(jnp.int32)
    adapter_pages = draw_adapter_pages(jax.random.fold_in(key_list[7], 71), 0)
    row_adapters = draw_row_adapters(jax.random.fold_in(key_list[7], 71), 0)
    return {"hidden_inputs": hidden_inputs, "base_matrix": base_matrix, "adapter_down": adapter_down, "adapter_up": adapter_up, "adapter_ranks": adapter_ranks, "adapter_pages": adapter_pages, "row_adapters": row_adapters}


def reference(hidden_inputs, base_matrix, adapter_down, adapter_up, adapter_ranks, adapter_pages, row_adapters):
    flat_rows = hidden_inputs.reshape(ROWS * STEPS, MODEL_WIDTH)
    base_output = jnp.dot(flat_rows, base_matrix, preferred_element_type=jnp.float32).reshape(ROWS, STEPS, MODEL_WIDTH)
    slot_for_row = adapter_pages[row_adapters].astype(jnp.int32)
    rank_vector = adapter_ranks[row_adapters].astype(jnp.int32)

    def single_row(items):
        features, page_slot_index, rank_value = items
        down_slot_page = adapter_down[page_slot_index].astype(jnp.float32)
        rank_sum = jnp.einsum("sd,rd->sr", features.astype(jnp.float32), down_slot_page)
        rank_mask = jnp.arange(MAXIMUM_RANK) < rank_value
        row_scale = 32.0 / rank_value.astype(jnp.float32)
        reduced = jnp.where(rank_mask[None, :], rank_sum * row_scale, 0.0).astype(jnp.bfloat16)
        up_slot_page = adapter_up[page_slot_index].astype(jnp.float32)
        return jnp.einsum("sr,rd->sd", reduced.astype(jnp.float32), up_slot_page).astype(jnp.bfloat16)

    adapter_output = lax.map(single_row, (hidden_inputs, slot_for_row, rank_vector))
    return (base_output + adapter_output.astype(jnp.float32)).astype(jnp.bfloat16)
```

```python
import jax
import jax.numpy as jnp
from jax import lax
from jax.sharding import PartitionSpec as P

SIDE = 4
BOTH = ("group", "tp")


def sign_of(core):
    return 1 if core == 0 else -1


def shift_pairs(dx, dy):
    pairs = []
    for group in range(8):
        sign = sign_of(group % 2)
        for x in range(SIDE):
            for y in range(SIDE):
                to = ((x + sign * dx) % SIDE) * SIDE + (y + sign * dy) % SIDE
                pairs.append((group * 16 + x * SIDE + y, group * 16 + to))
    return pairs


def shift(value, dx, dy):
    return lax.ppermute(value, BOTH, shift_pairs(dx, dy))


def gather_chunks(own):
    got = {(0, 0): own}
    got[1, 0] = shift(own, 1, 0)
    got[0, 1] = shift(own, 0, 1)
    got[-1, 0] = shift(own, -1, 0)
    got[0, -1] = shift(own, 0, -1)
    got[2, 0] = shift(got[1, 0], 1, 0)
    got[0, 2] = shift(got[0, 1], 0, 1)
    got[1, 1] = shift(got[0, 1], 1, 0)
    got[-1, 1] = shift(got[-1, 0], 0, 1)
    got[-1, -1] = shift(got[0, -1], -1, 0)
    got[1, -1] = shift(got[1, 0], 0, -1)
    got[1, 2] = shift(got[0, 2], 1, 0)
    got[-1, 2] = shift(got[0, 2], -1, 0)
    got[2, 1] = shift(got[2, 0], 0, 1)
    got[2, -1] = shift(got[2, 0], 0, -1)
    half = own.shape[0] // 2
    first = shift(got[1, 2][:half], 1, 0)
    second = shift(got[2, 1][half:], 0, 1)
    got[2, 2] = jnp.concatenate([first, second], axis=0)
    return got


def lookup(table, index):
    onehot = index[:, None] == jnp.arange(table.shape[0], dtype=jnp.int32)[None, :]
    return jnp.sum(jnp.where(onehot, table[None, :], 0), axis=1)


def per_device(
    hidden_inputs, base_matrix, adapter_down, adapter_up, adapter_ranks, adapter_pages, row_adapters
):
    row_count, steps, width = hidden_inputs.shape
    flat_count = row_count * steps
    tp_index = lax.axis_index("tp")
    sign = 1 - 2 * (lax.axis_index("group") % 2)
    place_x, place_y = tp_index // SIDE, tp_index % SIDE
    tp_size = SIDE * SIDE

    rows = hidden_inputs.reshape(flat_count, width)
    chunks = gather_chunks(rows)

    down_every = lax.all_gather(adapter_down, "group", axis=0, tiled=True)
    up_every = lax.all_gather(adapter_up, "group", axis=0, tiled=True)
    pages, rank_width = down_every.shape[:2]

    slot = jnp.repeat(lookup(adapter_pages, row_adapters), steps)
    rank = jnp.repeat(lookup(adapter_ranks, row_adapters), steps)
    picked = slot[:, None] == jnp.arange(pages, dtype=jnp.int32)[None, :]
    scores = lax.dot_general(
        rows,
        down_every.reshape(pages * rank_width, width),
        (((1,), (1,)), ((), ())),
        preferred_element_type=jnp.float32,
    ).reshape(flat_count, pages, rank_width)
    partial = jnp.sum(jnp.where(picked[:, :, None], scores, 0.0), axis=1)
    share = flat_count // tp_size
    parts = lax.all_to_all(
        partial.reshape(tp_size, share, rank_width), "tp", 0, 0, tiled=True
    )
    rank_sum = jnp.sum(parts, axis=0)
    own_rank = lax.dynamic_slice(rank, (tp_index * share,), (share,))
    mask = jnp.arange(rank_width, dtype=jnp.int32)[None, :] < own_rank[:, None]
    scale = 32.0 / own_rank.astype(jnp.float32)
    own_reduced = jnp.where(mask, rank_sum * scale[:, None], 0.0).astype(jnp.bfloat16)
    reduced = lax.all_to_all(
        jnp.broadcast_to(own_reduced[None], (tp_size, share, rank_width)), "tp", 0, 0, tiled=True
    ).reshape(flat_count, rank_width)
    spread = jnp.where(picked[:, :, None], reduced[:, None, :], jnp.zeros((), jnp.bfloat16))
    lora = jnp.dot(
        spread.reshape(flat_count, pages * rank_width),
        up_every.reshape(pages * rank_width, width),
        preferred_element_type=jnp.float32,
    ).astype(jnp.bfloat16)

    base = None
    for (dx, dy), chunk in chunks.items():
        source = ((place_x - sign * dx) % SIDE) * SIDE + (place_y - sign * dy) % SIDE
        block = lax.dynamic_slice(base_matrix, (source * width, 0), (width, base_matrix.shape[1]))
        term = jnp.dot(chunk, block, preferred_element_type=jnp.float32)
        base = term if base is None else base + term
    return (base + lora.astype(jnp.float32)).astype(jnp.bfloat16).reshape(hidden_inputs.shape)


def solution(mesh):
    return jax.shard_map(
        per_device,
        mesh=mesh,
        in_specs=(
            P("group", None, "tp"),
            P(None, "tp"),
            P("group", None, "tp"),
            P("group", None, "tp"),
            P(),
            P(),
            P("group"),
        ),
        out_specs=P("group", None, "tp"),
        check_vma=False,
    )
```

```python
import functools

import jax
import jax.numpy as jnp
from jax import lax
from jax.experimental import pallas as pl
from jax.experimental.pallas import tpu as pltpu
from jax.sharding import PartitionSpec as P

SIDE = 4
BOTH = ("group", "tp")
VMEM_BYTES = 28 * 2**20
DOWN_BLOCK = 16
UP_BLOCK = 32
AHEAD = 3
WINDOW = 4


def shift_pairs(dx, dy):
    pairs = []
    for group in range(8):
        step_x, step_y = (-dy, -dx) if group % 2 else (dx, dy)
        for x in range(SIDE):
            for y in range(SIDE):
                to = (x + step_x) % SIDE * SIDE + (y + step_y) % SIDE
                pairs.append((group * 16 + x * SIDE + y, group * 16 + to))
    return pairs


def shift(value, dx, dy):
    return lax.ppermute(value, BOTH, shift_pairs(dx, dy))


def after(value, *others):
    return lax.optimization_barrier((value,) + others)[0]


def in_vmem(value):
    return pltpu.with_memory_space_constraint(value, pltpu.VMEM)


class Messages:
    def __init__(self):
        self.sent = []

    def send(self, value, dx, dy, waits=()):
        earlier = self.sent[-WINDOW:][:1] if len(self.sent) >= WINDOW else []
        self.sent.append(shift(after(value, *earlier, *waits), dx, dy))
        return self.sent[-1]


def place_of(name):
    index = lax.axis_index("tp")
    core = lax.axis_index("group") & 1
    step_x = jnp.where(core == 1, -name[1], name[0])
    step_y = jnp.where(core == 1, -name[0], name[1])
    x = ((index >> 2) + SIDE - step_x) & (SIDE - 1)
    y = ((index & (SIDE - 1)) + SIDE - step_y) & (SIDE - 1)
    return x * SIDE + y


def local_call(body, name, operands, out_shape, flops=0, scratch=()):
    return pl.pallas_call(
        body,
        in_specs=[pl.BlockSpec(memory_space=pltpu.VMEM)] * len(operands),
        out_specs=jax.tree.map(lambda _: pl.BlockSpec(memory_space=pltpu.VMEM), out_shape),
        out_shape=out_shape,
        scratch_shapes=scratch,
        compiler_params=pltpu.CompilerParams(vmem_limit_bytes=VMEM_BYTES),
        cost_estimate=pl.CostEstimate(flops=flops, bytes_accessed=2**20, transcendentals=0),
        name=name,
    )(*[in_vmem(value) for value in operands])


def flatten_body(hidden_ref, rows_ref, first_ref, second_ref):
    rows = hidden_ref[...].reshape(rows_ref.shape)
    half = rows.shape[0] // 2
    rows_ref[...] = rows
    first_ref[...] = rows[:half]
    second_ref[...] = rows[half:]


def flatten(hidden):
    rows, steps, width = hidden.shape
    count = rows * steps
    shapes = [pltpu.VMEM((size, width), hidden.dtype) for size in (count, count // 2, count // 2)]
    return local_call(flatten_body, "flatten", [hidden], shapes)


def join_body(*refs):
    for i, ref in enumerate(refs[:-1]):
        refs[-1][i] = ref[...]


def join(parts):
    out_shape = jax.ShapeDtypeStruct((len(parts), *parts[0].shape), parts[0].dtype)
    return local_call(join_body, "join", parts, out_shape)


def base_body(halves, has_total, *refs):
    refs = list(refs)
    arrays = [[refs.pop(0) for _ in names] for names in halves]
    weight_ref = refs.pop(0)
    total_ref = refs.pop(0) if has_total else None
    out_ref, chunks, blocks, sems = refs
    width = blocks.shape[1]
    half = chunks.shape[1]

    jobs = []
    for h, (names, half_refs) in enumerate(zip(halves, arrays)):
        for places, ref in zip(names, half_refs):
            for i, place in enumerate(places):
                jobs.append((h, place, ref.at[i]))
    jobs.sort(key=lambda job: job[0])

    def copies(j):
        start = pl.multiple_of(place_of(jobs[j][1]) * width, width)
        block = weight_ref.at[pl.ds(start, width)]
        return (
            pltpu.make_async_copy(jobs[j][2], chunks.at[j], sems.at[j, 0]),
            pltpu.make_async_copy(block, blocks.at[j], sems.at[j, 1]),
        )

    held = [copies(j) for j in range(len(jobs))]
    for pair in held[:AHEAD]:
        for copy in pair:
            copy.start()
    for h in range(len(halves)):
        cut = pl.ds(h * half, half)
        total = total_ref[cut, :] if has_total else None
        for j, job in enumerate(jobs):
            if job[0] != h:
                continue
            for copy in held[j]:
                copy.wait()
            for pair in held[j + AHEAD : j + AHEAD + 1]:
                for copy in pair:
                    copy.start()
            term = jnp.dot(chunks[j], blocks[j], preferred_element_type=jnp.float32)
            total = term if total is None else total + term
        if out_ref.ndim == 3:
            part = out_ref.shape[0] // len(halves)
            shape = (part, *out_ref.shape[1:])
            out_ref[pl.ds(h * part, part)] = total.astype(out_ref.dtype).reshape(shape)
        else:
            out_ref[cut, :] = total


def in_hbm(value):
    return pltpu.with_memory_space_constraint(value, pltpu.HBM)


def base_dots(halves, weights, total, last=None):
    names = [[places for _, places in half] for half in halves]
    arrays = [in_hbm(array) for half in halves for array, _ in half]
    jobs = sum(len(places) for half in names for places in half)
    rows, width = arrays[0].shape[1:]
    columns = weights.shape[1]
    totals = [] if total is None else [in_vmem(total)]
    in_place = pl.BlockSpec(memory_space=pltpu.VMEM)
    return pl.pallas_call(
        functools.partial(base_body, names, total is not None),
        in_specs=[pl.BlockSpec(memory_space=pltpu.HBM)] * (len(arrays) + 1)
        + [in_place] * len(totals),
        out_specs=in_place,
        out_shape=pltpu.VMEM((2 * rows, columns), jnp.float32) if last is None else last,
        scratch_shapes=[
            pltpu.VMEM((jobs, rows, width), arrays[0].dtype),
            pltpu.VMEM((jobs, width, columns), weights.dtype),
            pltpu.SemaphoreType.DMA((jobs, 2)),
        ],
        compiler_params=pltpu.CompilerParams(vmem_limit_bytes=VMEM_BYTES),
        cost_estimate=pl.CostEstimate(
            flops=2 * rows * width * columns * jobs, bytes_accessed=2**20, transcendentals=0
        ),
        name="base_dots",
    )(*arrays, in_hbm(weights), *totals)


def flat_pages(pages):
    return in_hbm(pages.reshape(pages.shape[0] * pages.shape[1], pages.shape[2]))


def scores_body(rank_width, slot_ref, rows_ref, pages_ref, out_ref, sum_ref):
    step = pl.program_id(0)

    @pl.when(step == 0)
    def _():
        sum_ref[...] = jnp.zeros(sum_ref.shape, sum_ref.dtype)

    scores = lax.dot_general(
        pages_ref[...],
        rows_ref[...],
        (((1,), (1,)), ((), ())),
        preferred_element_type=jnp.float32,
    )
    slot = slot_ref[...] - step * DOWN_BLOCK
    partial = sum_ref[...]
    for s in range(DOWN_BLOCK):
        part = scores[s * rank_width : (s + 1) * rank_width]
        partial = partial + jnp.where(slot == s, part, 0.0)
    sum_ref[...] = partial

    @pl.when(step == pl.num_programs(0) - 1)
    def _():
        out_ref[...] = partial.reshape(out_ref.shape)


def rank_scores(slot, rows, down, shares):
    pages, rank_width, width = down.shape
    count = rows.shape[0]
    in_place = pl.BlockSpec(memory_space=pltpu.VMEM)
    return pl.pallas_call(
        functools.partial(scores_body, rank_width),
        grid=(pages // DOWN_BLOCK,),
        in_specs=[
            in_place,
            in_place,
            pl.BlockSpec((DOWN_BLOCK * rank_width, width), lambda i: (i, 0)),
        ],
        out_specs=in_place,
        out_shape=jax.ShapeDtypeStruct((shares, rank_width // shares, count), jnp.float32),
        scratch_shapes=[pltpu.VMEM((rank_width, count), jnp.float32)],
        compiler_params=pltpu.CompilerParams(vmem_limit_bytes=VMEM_BYTES),
        cost_estimate=pl.CostEstimate(
            flops=2 * count * width * pages * rank_width, bytes_accessed=5 * 2**20, transcendentals=0
        ),
        name="rank_scores",
    )(in_vmem(slot), in_vmem(rows), flat_pages(down))


def reduce_body(parts_ref, rank_ref, out_ref):
    shares, share, count = parts_ref.shape
    rank_sum = jnp.sum(parts_ref[...], axis=0)
    rank = rank_ref[...]
    own = lax.axis_index("tp") * share + lax.broadcasted_iota(jnp.int32, (share, count), 0)
    scale = 32.0 / rank.astype(jnp.float32)
    reduced = jnp.where(own < rank, rank_sum * scale, 0.0).astype(out_ref.dtype)
    out_ref[...] = jnp.broadcast_to(reduced[None], out_ref.shape)


def reduce_ranks(parts, rank):
    return local_call(
        reduce_body, "reduce_ranks", [parts, rank], jax.ShapeDtypeStruct(parts.shape, jnp.bfloat16)
    )


def up_body(rank_width, slot_ref, reduced_ref, pages_ref, total_ref, out_ref, lora_ref, pair_ref):
    step = pl.program_id(0)

    @pl.when(step == 0)
    def _():
        reduced = reduced_ref[...].astype(jnp.float32).reshape(rank_width, -1)
        pair_ref[...] = jnp.concatenate([reduced, reduced], axis=0).T.astype(pair_ref.dtype)

    lane_slot = lax.broadcasted_iota(jnp.int32, pair_ref.shape, 1) // rank_width
    slot = slot_ref[...] - step * UP_BLOCK - lane_slot
    reduced = pair_ref[...]
    zero = jnp.zeros((), reduced.dtype)
    spread = jnp.concatenate(
        [jnp.where(slot == s, reduced, zero) for s in range(0, UP_BLOCK, 2)], axis=1
    )
    part = jnp.dot(spread, pages_ref[...], preferred_element_type=jnp.float32)

    @pl.when(step == 0)
    def _():
        lora_ref[...] = part

    @pl.when((step > 0) & (step < pl.num_programs(0) - 1))
    def _():
        lora_ref[...] += part

    @pl.when(step == pl.num_programs(0) - 1)
    def _():
        lora = lora_ref[...] + part
        out_ref[...] = total_ref[...] + lora.astype(jnp.bfloat16).astype(jnp.float32)


def add_lora(slot, reduced, up, total):
    pages, rank_width, width = up.shape
    count = total.shape[0]
    in_place = pl.BlockSpec(memory_space=pltpu.VMEM)
    return pl.pallas_call(
        functools.partial(up_body, rank_width),
        grid=(pages // UP_BLOCK,),
        in_specs=[
            in_place,
            in_place,
            pl.BlockSpec((UP_BLOCK * rank_width, width), lambda i: (i, 0)),
            in_place,
        ],
        out_specs=in_place,
        out_shape=pltpu.VMEM((count, width), jnp.float32),
        scratch_shapes=[
            pltpu.VMEM((count, width), jnp.float32),
            pltpu.VMEM((count, 2 * rank_width), jnp.bfloat16),
        ],
        compiler_params=pltpu.CompilerParams(vmem_limit_bytes=VMEM_BYTES),
        cost_estimate=pl.CostEstimate(
            flops=2 * count * width * pages * rank_width, bytes_accessed=8 * 2**20, transcendentals=0
        ),
        name="add_lora",
    )(in_vmem(slot), in_vmem(reduced), flat_pages(up), in_vmem(total))


def lookup(table, index):
    onehot = index[:, None] == jnp.arange(table.shape[0], dtype=jnp.int32)[None, :]
    return jnp.sum(jnp.where(onehot, table[None, :], 0), axis=1)


def per_device(
    hidden_inputs, base_matrix, adapter_down, adapter_up, adapter_ranks, adapter_pages, row_adapters
):
    row_count, steps, width = hidden_inputs.shape
    flat_count = row_count * steps
    tp_size = SIDE * SIDE

    rows, first, second = flatten(hidden_inputs)
    down = lax.all_gather(adapter_down, "group", axis=0, tiled=True)
    up = lax.all_gather(after(adapter_up, adapter_down), "group", axis=0, tiled=True)
    slot = jnp.repeat(lookup(adapter_pages, row_adapters), steps)
    rank = jnp.repeat(lookup(adapter_ranks, row_adapters), steps)

    send = Messages().send
    first_1 = send(first, 1, 0)
    second_1 = send(second, 0, 1)
    first_3 = send(first, -1, 0)
    second_3 = send(second, 0, -1)
    first_2 = send(first_1, 1, 0)
    second_2 = send(second_1, 0, 1)
    line = (0, 1, -1, 2)
    first_line = join([first, first_1, first_3, first_2])
    second_line = join([second, second_1, second_3, second_2])

    def both(first_part, second_part, step):
        return [
            [(first_part, [(along, step) for along in line])],
            [(second_part, [(step, along) for along in line])],
        ]

    first_ahead = send(first_line, 0, 1)
    second_ahead = send(second_line, 1, 0)
    total = base_dots(both(first_line, second_line, 0), base_matrix, None)
    first_back = send(first_line, 0, -1, waits=[total])
    second_back = send(second_line, -1, 0)
    partial = rank_scores(slot[None, :], rows, down, tp_size)
    parts = lax.all_to_all(partial, "tp", 0, 0, tiled=True)
    first_far = send(first_ahead, 0, 1, waits=[parts])
    second_far = send(second_ahead, 1, 0)
    reduced = lax.all_to_all(reduce_ranks(parts, rank[None, :]), "tp", 0, 0, tiled=True)
    total = base_dots(both(first_ahead, second_ahead, 1), base_matrix, total)
    total = base_dots(both(first_back, second_back, -1), base_matrix, total)
    total = add_lora(slot[:, None], reduced, up, total)
    last = jax.ShapeDtypeStruct(hidden_inputs.shape, hidden_inputs.dtype)
    return base_dots(both(first_far, second_far, 2), base_matrix, total, last)


def solution(mesh):
    return jax.shard_map(
        per_device,
        mesh=mesh,
        in_specs=(
            P("group", None, "tp"),
            P(None, "tp"),
            P("group", None, "tp"),
            P("group", None, "tp"),
            P(),
            P(),
            P("group"),
        ),
        out_specs=P("group", None, "tp"),
        check_vma=False,
    )
```

```python
import functools

import jax
import jax.numpy as jnp
from jax import lax
from jax.experimental import pallas as pl
from jax.experimental.pallas import tpu as pltpu
from jax.sharding import PartitionSpec as P

SIDE = 4
BOTH = ("group", "tp")
VMEM_BYTES = 28 * 2**20
DOWN_BLOCK = 16
UP_BLOCK = 32
AHEAD = 6
WINDOW = 4


def shift_pairs(dx, dy):
    pairs = []
    for group in range(8):
        step_x, step_y = (-dy, -dx) if group % 2 else (dx, dy)
        for x in range(SIDE):
            for y in range(SIDE):
                to = (x + step_x) % SIDE * SIDE + (y + step_y) % SIDE
                pairs.append((group * 16 + x * SIDE + y, group * 16 + to))
    return pairs


def shift(value, dx, dy):
    return lax.ppermute(value, BOTH, shift_pairs(dx, dy))


def after(value, *others):
    return lax.optimization_barrier((value,) + others)[0]


def in_vmem(value):
    return pltpu.with_memory_space_constraint(value, pltpu.VMEM)


class Messages:
    def __init__(self):
        self.sent = []

    def send(self, value, dx, dy, waits=()):
        earlier = self.sent[-WINDOW:][:1] if len(self.sent) >= WINDOW else []
        self.sent.append(shift(after(value, *earlier, *waits), dx, dy))
        return self.sent[-1]


def place_of(name):
    index = lax.axis_index("tp")
    core = lax.axis_index("group") & 1
    step_x = jnp.where(core == 1, -name[1], name[0])
    step_y = jnp.where(core == 1, -name[0], name[1])
    x = ((index >> 2) + SIDE - step_x) & (SIDE - 1)
    y = ((index & (SIDE - 1)) + SIDE - step_y) & (SIDE - 1)
    return x * SIDE + y


def local_call(body, name, operands, out_shape, flops=0, scratch=()):
    return pl.pallas_call(
        body,
        in_specs=[pl.BlockSpec(memory_space=pltpu.VMEM)] * len(operands),
        out_specs=jax.tree.map(lambda _: pl.BlockSpec(memory_space=pltpu.VMEM), out_shape),
        out_shape=out_shape,
        scratch_shapes=scratch,
        compiler_params=pltpu.CompilerParams(vmem_limit_bytes=VMEM_BYTES),
        cost_estimate=pl.CostEstimate(flops=flops, bytes_accessed=2**20, transcendentals=0),
        name=name,
    )(*[in_vmem(value) for value in operands])


def flatten_body(hidden_ref, rows_ref, first_ref, second_ref):
    rows = hidden_ref[...].reshape(rows_ref.shape)
    half = rows.shape[0] // 2
    rows_ref[...] = rows
    first_ref[...] = rows[:half]
    second_ref[...] = rows[half:]


def flatten(hidden):
    rows, steps, width = hidden.shape
    count = rows * steps
    shapes = [pltpu.VMEM((size, width), hidden.dtype) for size in (count, count // 2, count // 2)]
    return local_call(flatten_body, "flatten", [hidden], shapes)


def join_body(*refs):
    for i, ref in enumerate(refs[:-1]):
        refs[-1][i] = ref[...]


def join(parts):
    out_shape = jax.ShapeDtypeStruct((len(parts), *parts[0].shape), parts[0].dtype)
    return local_call(join_body, "join", parts, out_shape)


def base_body(halves, has_total, *refs):
    refs = list(refs)
    arrays = [[refs.pop(0) for _ in names] for names in halves]
    weight_ref = refs.pop(0)
    total_ref = refs.pop(0) if has_total else None
    out_ref, chunks, blocks, sems = refs
    width = blocks.shape[1]
    half = chunks.shape[1]

    jobs = []
    for h, (names, half_refs) in enumerate(zip(halves, arrays)):
        for places, ref in zip(names, half_refs):
            for i, place in enumerate(places):
                jobs.append((h, place, ref.at[i]))
    jobs.sort(key=lambda job: job[0])

    def copies(j):
        start = pl.multiple_of(place_of(jobs[j][1]) * width, width)
        block = weight_ref.at[pl.ds(start, width)]
        return (
            pltpu.make_async_copy(jobs[j][2], chunks.at[j], sems.at[j, 0]),
            pltpu.make_async_copy(block, blocks.at[j], sems.at[j, 1]),
        )

    held = [copies(j) for j in range(len(jobs))]
    for pair in held[:AHEAD]:
        for copy in pair:
            copy.start()
    for h in range(len(halves)):
        cut = pl.ds(h * half, half)
        total = total_ref[cut, :] if has_total else None
        for j, job in enumerate(jobs):
            if job[0] != h:
                continue
            for copy in held[j]:
                copy.wait()
            for pair in held[j + AHEAD : j + AHEAD + 1]:
                for copy in pair:
                    copy.start()
            term = jnp.dot(chunks[j], blocks[j], preferred_element_type=jnp.float32)
            total = term if total is None else total + term
        if out_ref.ndim == 3:
            part = out_ref.shape[0] // len(halves)
            shape = (part, *out_ref.shape[1:])
            out_ref[pl.ds(h * part, part)] = total.astype(out_ref.dtype).reshape(shape)
        else:
            out_ref[cut, :] = total


def in_hbm(value):
    return pltpu.with_memory_space_constraint(value, pltpu.HBM)


def base_dots(halves, weights, total, last=None):
    names = [[places for _, places in half] for half in halves]
    arrays = [in_hbm(array) for half in halves for array, _ in half]
    jobs = sum(len(places) for half in names for places in half)
    rows, width = arrays[0].shape[1:]
    columns = weights.shape[1]
    totals = [] if total is None else [in_vmem(total)]
    in_place = pl.BlockSpec(memory_space=pltpu.VMEM)
    return pl.pallas_call(
        functools.partial(base_body, names, total is not None),
        in_specs=[pl.BlockSpec(memory_space=pltpu.HBM)] * (len(arrays) + 1)
        + [in_place] * len(totals),
        out_specs=in_place,
        out_shape=pltpu.VMEM((2 * rows, columns), jnp.float32) if last is None else last,
        scratch_shapes=[
            pltpu.VMEM((jobs, rows, width), arrays[0].dtype),
            pltpu.VMEM((jobs, width, columns), weights.dtype),
            pltpu.SemaphoreType.DMA((jobs, 2)),
        ],
        compiler_params=pltpu.CompilerParams(vmem_limit_bytes=VMEM_BYTES),
        cost_estimate=pl.CostEstimate(
            flops=2 * rows * width * columns * jobs, bytes_accessed=2**20, transcendentals=0
        ),
        name="base_dots",
    )(*arrays, in_hbm(weights), *totals)


def flat_pages(pages):
    return in_hbm(pages.reshape(pages.shape[0] * pages.shape[1], pages.shape[2]))


def scores_body(rank_width, slot_ref, rows_ref, pages_ref, out_ref, sum_ref):
    step = pl.program_id(0)

    @pl.when(step == 0)
    def _():
        sum_ref[...] = jnp.zeros(sum_ref.shape, sum_ref.dtype)

    scores = lax.dot_general(
        pages_ref[...],
        rows_ref[...],
        (((1,), (1,)), ((), ())),
        preferred_element_type=jnp.float32,
    )
    slot = slot_ref[...] - step * DOWN_BLOCK
    partial = sum_ref[...]
    for s in range(DOWN_BLOCK):
        part = scores[s * rank_width : (s + 1) * rank_width]
        partial = partial + jnp.where(slot == s, part, 0.0)
    sum_ref[...] = partial

    @pl.when(step == pl.num_programs(0) - 1)
    def _():
        out_ref[...] = partial.reshape(out_ref.shape)


def rank_scores(slot, rows, down, shares):
    pages, rank_width, width = down.shape
    count = rows.shape[0]
    in_place = pl.BlockSpec(memory_space=pltpu.VMEM)
    return pl.pallas_call(
        functools.partial(scores_body, rank_width),
        grid=(pages // DOWN_BLOCK,),
        in_specs=[
            in_place,
            pl.BlockSpec((count, width), lambda i: (0, 0)),
            pl.BlockSpec((DOWN_BLOCK * rank_width, width), lambda i: (i, 0)),
        ],
        out_specs=in_place,
        out_shape=jax.ShapeDtypeStruct((shares, rank_width // shares, count), jnp.float32),
        scratch_shapes=[pltpu.VMEM((rank_width, count), jnp.float32)],
        compiler_params=pltpu.CompilerParams(vmem_limit_bytes=VMEM_BYTES),
        cost_estimate=pl.CostEstimate(
            flops=2 * count * width * pages * rank_width, bytes_accessed=5 * 2**20, transcendentals=0
        ),
        name="rank_scores",
    )(in_vmem(slot), in_hbm(rows), flat_pages(down))


def reduce_body(parts_ref, rank_ref, out_ref):
    shares, share, count = parts_ref.shape
    rank_sum = jnp.sum(parts_ref[...], axis=0)
    rank = rank_ref[...]
    own = lax.axis_index("tp") * share + lax.broadcasted_iota(jnp.int32, (share, count), 0)
    scale = 32.0 / rank.astype(jnp.float32)
    reduced = jnp.where(own < rank, rank_sum * scale, 0.0).astype(out_ref.dtype)
    out_ref[...] = jnp.broadcast_to(reduced[None], out_ref.shape)


def reduce_ranks(parts, rank):
    return local_call(
        reduce_body, "reduce_ranks", [parts, rank], jax.ShapeDtypeStruct(parts.shape, jnp.bfloat16)
    )


def up_body(rank_width, slot_ref, reduced_ref, pages_ref, total_ref, out_ref):
    reduced = reduced_ref[...].astype(jnp.float32).reshape(rank_width, -1)
    pair = jnp.concatenate([reduced, reduced], axis=0).T.astype(reduced_ref.dtype)
    slot = slot_ref[...] - lax.broadcasted_iota(jnp.int32, pair.shape, 1) // rank_width
    zero = jnp.zeros((), pair.dtype)
    depth = UP_BLOCK * rank_width
    lora = None
    for i in range(pages_ref.shape[0] // depth):
        first = i * UP_BLOCK
        spread = jnp.concatenate(
            [jnp.where(slot == first + s, pair, zero) for s in range(0, UP_BLOCK, 2)], axis=1
        )
        pages = pages_ref[pl.ds(i * depth, depth), :]
        part = jnp.dot(spread, pages, preferred_element_type=jnp.float32)
        lora = part if lora is None else lora + part
    out_ref[...] = total_ref[...] + lora.astype(jnp.bfloat16).astype(jnp.float32)


def add_lora(slot, reduced, up, total):
    pages, rank_width, width = up.shape
    count = total.shape[0]
    return local_call(
        functools.partial(up_body, rank_width),
        "add_lora",
        [slot, reduced, up.reshape(pages * rank_width, width), total],
        pltpu.VMEM((count, width), jnp.float32),
        flops=2 * count * width * pages * rank_width,
    )


def lookup(table, index):
    onehot = index[:, None] == jnp.arange(table.shape[0], dtype=jnp.int32)[None, :]
    return jnp.sum(jnp.where(onehot, table[None, :], 0), axis=1)


def per_device(
    hidden_inputs, base_matrix, adapter_down, adapter_up, adapter_ranks, adapter_pages, row_adapters
):
    row_count, steps, width = hidden_inputs.shape
    flat_count = row_count * steps
    tp_size = SIDE * SIDE

    rows, first, second = flatten(hidden_inputs)
    down = lax.all_gather(adapter_down, "group", axis=0, tiled=True)
    up = lax.all_gather(after(adapter_up, adapter_down), "group", axis=0, tiled=True)
    slot = jnp.repeat(lookup(adapter_pages, row_adapters), steps)
    rank = jnp.repeat(lookup(adapter_ranks, row_adapters), steps)

    send = Messages().send
    first_1 = send(first, 1, 0)
    second_1 = send(second, 0, 1)
    first_3 = send(first, -1, 0)
    second_3 = send(second, 0, -1)
    first_2 = send(first_1, 1, 0)
    second_2 = send(second_1, 0, 1)
    line = (0, 1, -1, 2)
    first_line = join([first, first_1, first_3, first_2])
    second_line = join([second, second_1, second_3, second_2])

    def both(first_part, second_part, step):
        return [
            [(first_part, [(along, step) for along in line])],
            [(second_part, [(step, along) for along in line])],
        ]

    first_ahead = send(first_line, 0, 1)
    second_ahead = send(second_line, 1, 0)
    total = base_dots(both(first_line, second_line, 0), base_matrix, None)
    first_back = send(first_line, 0, -1, waits=[total])
    second_back = send(second_line, -1, 0)
    partial = rank_scores(slot[None, :], rows, down, tp_size)
    parts = lax.all_to_all(partial, "tp", 0, 0, tiled=True)
    first_far = send(first_ahead, 0, 1, waits=[parts])
    second_far = send(second_ahead, 1, 0)
    spread = reduce_ranks(parts, rank[None, :])
    reduced = lax.all_to_all(spread, "tp", 0, 0, tiled=True)
    total = base_dots(both(first_ahead, second_ahead, 1), base_matrix, after(total, spread))
    total = base_dots(both(first_back, second_back, -1), base_matrix, total)
    total = add_lora(slot[:, None], reduced, up, total)
    last = jax.ShapeDtypeStruct(hidden_inputs.shape, hidden_inputs.dtype)
    return base_dots(both(first_far, second_far, 2), base_matrix, total, last)


def solution(mesh):
    return jax.shard_map(
        per_device,
        mesh=mesh,
        in_specs=(
            P("group", None, "tp"),
            P(None, "tp"),
            P("group", None, "tp"),
            P("group", None, "tp"),
            P(),
            P(),
            P("group"),
        ),
        out_specs=P("group", None, "tp"),
        check_vma=False,
    )
```

```python
import functools

import jax
import jax.numpy as jnp
from jax import lax
from jax.experimental import pallas as pl
from jax.experimental.pallas import tpu as pltpu
from jax.sharding import PartitionSpec as P

SIDE = 4
BOTH = ("group", "tp")
VMEM_BYTES = 28 * 2**20
DOWN_BLOCK = 16
UP_BLOCK = 32
AHEAD = 6
WINDOW = 4


def shift_pairs(dx, dy):
    pairs = []
    for group in range(8):
        step_x, step_y = (-dy, -dx) if group % 2 else (dx, dy)
        for x in range(SIDE):
            for y in range(SIDE):
                to = (x + step_x) % SIDE * SIDE + (y + step_y) % SIDE
                pairs.append((group * 16 + x * SIDE + y, group * 16 + to))
    return pairs


def shift(value, dx, dy):
    return lax.ppermute(value, BOTH, shift_pairs(dx, dy))


def after(value, *others):
    return lax.optimization_barrier((value,) + others)[0]


def in_vmem(value):
    return pltpu.with_memory_space_constraint(value, pltpu.VMEM)


class Messages:
    def __init__(self):
        self.sent = []

    def send(self, value, dx, dy, waits=()):
        earlier = self.sent[-WINDOW:][:1] if len(self.sent) >= WINDOW else []
        self.sent.append(shift(after(value, *earlier, *waits), dx, dy))
        return self.sent[-1]


def place_of(name):
    index = lax.axis_index("tp")
    core = lax.axis_index("group") & 1
    step_x = jnp.where(core == 1, -name[1], name[0])
    step_y = jnp.where(core == 1, -name[0], name[1])
    x = ((index >> 2) + SIDE - step_x) & (SIDE - 1)
    y = ((index & (SIDE - 1)) + SIDE - step_y) & (SIDE - 1)
    return x * SIDE + y


def local_call(body, name, operands, out_shape, flops=0, scratch=()):
    return pl.pallas_call(
        body,
        in_specs=[pl.BlockSpec(memory_space=pltpu.VMEM)] * len(operands),
        out_specs=jax.tree.map(lambda _: pl.BlockSpec(memory_space=pltpu.VMEM), out_shape),
        out_shape=out_shape,
        scratch_shapes=scratch,
        compiler_params=pltpu.CompilerParams(vmem_limit_bytes=VMEM_BYTES),
        cost_estimate=pl.CostEstimate(flops=flops, bytes_accessed=2**20, transcendentals=0),
        name=name,
    )(*[in_vmem(value) for value in operands])


def flatten_body(hidden_ref, rows_ref, first_ref, second_ref):
    rows = hidden_ref[...].reshape(rows_ref.shape)
    half = rows.shape[0] // 2
    rows_ref[...] = rows
    first_ref[...] = rows[:half]
    second_ref[...] = rows[half:]


def flatten(hidden):
    rows, steps, width = hidden.shape
    count = rows * steps
    shapes = [pltpu.VMEM((size, width), hidden.dtype) for size in (count, count // 2, count // 2)]
    return local_call(flatten_body, "flatten", [hidden], shapes)


def join_body(*refs):
    for i, ref in enumerate(refs[:-1]):
        refs[-1][i] = ref[...]


def join(parts):
    out_shape = jax.ShapeDtypeStruct((len(parts), *parts[0].shape), parts[0].dtype)
    return local_call(join_body, "join", parts, out_shape)


def base_body(halves, has_total, *refs):
    refs = list(refs)
    arrays = [[refs.pop(0) for _ in names] for names in halves]
    weight_ref = refs.pop(0)
    total_ref = refs.pop(0) if has_total else None
    out_ref, chunks, blocks, sems = refs
    width = blocks.shape[1]
    half = chunks.shape[1]

    jobs = []
    for h, (names, half_refs) in enumerate(zip(halves, arrays)):
        for places, ref in zip(names, half_refs):
            for i, place in enumerate(places):
                jobs.append((h, place, ref.at[i]))
    jobs.sort(key=lambda job: job[0])

    def copies(j):
        start = pl.multiple_of(place_of(jobs[j][1]) * width, width)
        block = weight_ref.at[pl.ds(start, width)]
        return (
            pltpu.make_async_copy(jobs[j][2], chunks.at[j], sems.at[j, 0]),
            pltpu.make_async_copy(block, blocks.at[j], sems.at[j, 1]),
        )

    held = [copies(j) for j in range(len(jobs))]
    for pair in held[:AHEAD]:
        for copy in pair:
            copy.start()
    for h in range(len(halves)):
        cut = pl.ds(h * half, half)
        total = total_ref[cut, :] if has_total else None
        for j, job in enumerate(jobs):
            if job[0] != h:
                continue
            for copy in held[j]:
                copy.wait()
            for pair in held[j + AHEAD : j + AHEAD + 1]:
                for copy in pair:
                    copy.start()
            term = jnp.dot(chunks[j], blocks[j], preferred_element_type=jnp.float32)
            total = term if total is None else total + term
        if out_ref.ndim == 3:
            part = out_ref.shape[0] // len(halves)
            shape = (part, *out_ref.shape[1:])
            out_ref[pl.ds(h * part, part)] = total.astype(out_ref.dtype).reshape(shape)
        else:
            out_ref[cut, :] = total


def in_hbm(value):
    return pltpu.with_memory_space_constraint(value, pltpu.HBM)


def base_dots(halves, weights, total, last=None):
    names = [[places for _, places in half] for half in halves]
    arrays = [in_hbm(array) for half in halves for array, _ in half]
    jobs = sum(len(places) for half in names for places in half)
    rows, width = arrays[0].shape[1:]
    columns = weights.shape[1]
    totals = [] if total is None else [in_vmem(total)]
    in_place = pl.BlockSpec(memory_space=pltpu.VMEM)
    return pl.pallas_call(
        functools.partial(base_body, names, total is not None),
        in_specs=[pl.BlockSpec(memory_space=pltpu.HBM)] * (len(arrays) + 1)
        + [in_place] * len(totals),
        out_specs=in_place,
        out_shape=pltpu.VMEM((2 * rows, columns), jnp.float32) if last is None else last,
        scratch_shapes=[
            pltpu.VMEM((jobs, rows, width), arrays[0].dtype),
            pltpu.VMEM((jobs, width, columns), weights.dtype),
            pltpu.SemaphoreType.DMA((jobs, 2)),
        ],
        compiler_params=pltpu.CompilerParams(vmem_limit_bytes=VMEM_BYTES),
        cost_estimate=pl.CostEstimate(
            flops=2 * rows * width * columns * jobs, bytes_accessed=2**20, transcendentals=0
        ),
        name="base_dots",
    )(*arrays, in_hbm(weights), *totals)


def flat_pages(pages):
    return in_hbm(pages.reshape(pages.shape[0] * pages.shape[1], pages.shape[2]))


def scores_body(rank_width, slot_ref, rows_ref, pages_ref, out_ref, sum_ref):
    step = pl.program_id(0)

    @pl.when(step == 0)
    def _():
        sum_ref[...] = jnp.zeros(sum_ref.shape, sum_ref.dtype)

    scores = lax.dot_general(
        pages_ref[...],
        rows_ref[...],
        (((1,), (1,)), ((), ())),
        preferred_element_type=jnp.float32,
    )
    slot = slot_ref[...] - step * DOWN_BLOCK
    partial = sum_ref[...]
    for s in range(DOWN_BLOCK):
        part = scores[s * rank_width : (s + 1) * rank_width]
        partial = partial + jnp.where(slot == s, part, 0.0)
    sum_ref[...] = partial

    @pl.when(step == pl.num_programs(0) - 1)
    def _():
        out_ref[...] = partial.reshape(out_ref.shape)


def rank_scores(slot, rows, down, shares):
    pages, rank_width, width = down.shape
    count = rows.shape[0]
    in_place = pl.BlockSpec(memory_space=pltpu.VMEM)
    return pl.pallas_call(
        functools.partial(scores_body, rank_width),
        grid=(pages // DOWN_BLOCK,),
        in_specs=[
            in_place,
            pl.BlockSpec((count, width), lambda i: (0, 0)),
            pl.BlockSpec((DOWN_BLOCK * rank_width, width), lambda i: (i, 0)),
        ],
        out_specs=in_place,
        out_shape=jax.ShapeDtypeStruct((shares, rank_width // shares, count), jnp.float32),
        scratch_shapes=[pltpu.VMEM((rank_width, count), jnp.float32)],
        compiler_params=pltpu.CompilerParams(vmem_limit_bytes=VMEM_BYTES),
        cost_estimate=pl.CostEstimate(
            flops=2 * count * width * pages * rank_width, bytes_accessed=5 * 2**20, transcendentals=0
        ),
        name="rank_scores",
    )(in_vmem(slot), in_hbm(rows), flat_pages(down))


def reduce_body(parts_ref, rank_ref, out_ref):
    shares, share, count = parts_ref.shape
    rank_sum = jnp.sum(parts_ref[...], axis=0)
    rank = rank_ref[...]
    own = lax.axis_index("tp") * share + lax.broadcasted_iota(jnp.int32, (share, count), 0)
    scale = 32.0 / rank.astype(jnp.float32)
    reduced = jnp.where(own < rank, rank_sum * scale, 0.0).astype(out_ref.dtype)
    out_ref[...] = jnp.broadcast_to(reduced[None], out_ref.shape)


def reduce_ranks(parts, rank):
    return local_call(
        reduce_body, "reduce_ranks", [parts, rank], jax.ShapeDtypeStruct(parts.shape, jnp.bfloat16)
    )


def up_body(rank_width, slot_ref, reduced_ref, pages_ref, total_ref, out_ref):
    reduced = reduced_ref[...].astype(jnp.float32).reshape(rank_width, -1)
    pair = jnp.concatenate([reduced, reduced], axis=0).T.astype(reduced_ref.dtype)
    slot = slot_ref[...] - lax.broadcasted_iota(jnp.int32, pair.shape, 1) // rank_width
    zero = jnp.zeros((), pair.dtype)
    depth = UP_BLOCK * rank_width
    lora = None
    for i in range(pages_ref.shape[0] // depth):
        first = i * UP_BLOCK
        spread = jnp.concatenate(
            [jnp.where(slot == first + s, pair, zero) for s in range(0, UP_BLOCK, 2)], axis=1
        )
        pages = pages_ref[pl.ds(i * depth, depth), :]
        part = jnp.dot(spread, pages, preferred_element_type=jnp.float32)
        lora = part if lora is None else lora + part
    out_ref[...] = total_ref[...] + lora.astype(jnp.bfloat16).astype(jnp.float32)


def add_lora(slot, reduced, up, total):
    pages, rank_width, width = up.shape
    count = total.shape[0]
    return local_call(
        functools.partial(up_body, rank_width),
        "add_lora",
        [slot, reduced, up.reshape(pages * rank_width, width), total],
        pltpu.VMEM((count, width), jnp.float32),
        flops=2 * count * width * pages * rank_width,
    )


def lookup(table, index):
    onehot = index[:, None] == jnp.arange(table.shape[0], dtype=jnp.int32)[None, :]
    return jnp.sum(jnp.where(onehot, table[None, :], 0), axis=1)


def per_device(
    hidden_inputs, base_matrix, adapter_down, adapter_up, adapter_ranks, adapter_pages, row_adapters
):
    row_count, steps, width = hidden_inputs.shape
    flat_count = row_count * steps
    tp_size = SIDE * SIDE

    rows, first, second = flatten(hidden_inputs)
    down = lax.all_gather(adapter_down, "group", axis=0, tiled=True)
    up = lax.all_gather(after(adapter_up, adapter_down), "group", axis=0, tiled=True)
    slot = jnp.repeat(lookup(adapter_pages, row_adapters), steps)
    rank = jnp.repeat(lookup(adapter_ranks, row_adapters), steps)

    send = Messages().send
    first_1 = send(first, 1, 0)
    second_1 = send(second, 0, 1)
    first_3 = send(first, -1, 0)
    second_3 = send(second, 0, -1)
    first_2 = send(first_1, 1, 0)
    second_2 = send(second_1, 0, 1)
    line = (0, 1, -1, 2)
    first_line = join([first, first_1, first_3, first_2])
    second_line = join([second, second_1, second_3, second_2])

    def both(first_part, second_part, step):
        return [
            [(first_part, [(along, step) for along in line])],
            [(second_part, [(step, along) for along in line])],
        ]

    first_ahead = send(first_line, 0, 1)
    second_ahead = send(second_line, 1, 0)
    total = base_dots(both(first_line, second_line, 0), base_matrix, None)
    first_back = send(first_line, 0, -1)
    second_back = send(second_line, -1, 0)
    partial = rank_scores(slot[None, :], rows, down, tp_size)
    parts = lax.all_to_all(partial, "tp", 0, 0, tiled=True)
    first_far = send(first_ahead, 0, 1, waits=[parts])
    second_far = send(second_ahead, 1, 0)
    spread = reduce_ranks(parts, rank[None, :])
    reduced = lax.all_to_all(spread, "tp", 0, 0, tiled=True)
    total = base_dots(both(first_ahead, second_ahead, 1), base_matrix, after(total, spread))
    total = base_dots(both(first_back, second_back, -1), base_matrix, total)
    total = add_lora(slot[:, None], reduced, up, total)
    last = jax.ShapeDtypeStruct(hidden_inputs.shape, hidden_inputs.dtype)
    return base_dots(both(first_far, second_far, 2), base_matrix, total, last)


def solution(mesh):
    return jax.shard_map(
        per_device,
        mesh=mesh,
        in_specs=(
            P("group", None, "tp"),
            P(None, "tp"),
            P("group", None, "tp"),
            P("group", None, "tp"),
            P(),
            P(),
            P("group"),
        ),
        out_specs=P("group", None, "tp"),
        check_vma=False,
    )
```
